256 devices in a mesh: span: 8 (over x_lo, y), seq: 32 (over x_hi, z, core).
Axes of the slice: x: 4 (x_hi: 2, x_lo: 2; x = x_hi * 2 + x_lo), y: 4, z: 8, core: 2. Of those that a mesh axis runs over, the one named last changes fastest.
Arguments:
- noisy_qkv: bfloat16 [8, 1280, 3, 4096], P('span', 'seq'), may hold values from -20 to 20
- clean_cache: bfloat16 [8, 1280, 2, 4096], P('span', 'seq'), may hold values from -6 to 6
- span_ids: int32 [8], P('span'), may hold values from 0 to 7, each once
- sign_bits: int32 [128], replicated, may hold values 0 or 1
Outputs:
- attended: bfloat16 [8, 1280, 4096], P('span', 'seq')
The draws below stay inside these ranges and needn't reach their ends.
All inputs are finite; a program needn't handle non-finite values.
Results may differ from the reference program's by a relative error of at most 0.007.
Values may be sent and summed in bfloat16 or wider, within the bound.
A program may use at most 128 MiB of HBM per device.

```python
import math
import jax
import jax.numpy as jnp
from jax import lax

HD = 128
HEADS = 32
WIDTH = 4096
SPAN_TOK = 1280
N_SPAN = 8


def draw_noisy_qkv(key, part):
    key = jax.random.fold_in(key, 11)
    full_shape = (N_SPAN, SPAN_TOK, 3, WIDTH)
    return jax.random.normal(key, full_shape, jnp.float32).astype(jnp.bfloat16)


def touch_ends(drawn, stream_key, smallest, largest):
    longest = drawn.shape.index(max(drawn.shape))
    spots = []
    for shift in (0, 1):
        where = [jax.random.randint(jax.random.fold_in(stream_key, axis), (), 0, length) for axis, length in enumerate(drawn.shape)]
        where[longest] = (where[longest] + shift) % drawn.shape[longest]
        spots.append(tuple(where))
    return drawn.at[spots[0]].set(smallest).at[spots[1]].set(largest)


def steps_of(key, shape, pieces, low, top_value):
    loudness, own = 1.0, jax.random.fold_in(key, 6)
    for dim, shards_of in pieces:
        steps = jnp.exp(jax.random.uniform(jax.random.fold_in(own, dim), (shards_of,), jnp.float32, low / len(pieces), top_value / len(pieces)))
        loudness = loudness * jnp.repeat(steps, shape[dim] // shards_of).reshape([-1 if axis == dim else 1 for axis in range(len(shape))])
    return loudness


def gaussian(rng, shape, spread, limit, pieces=(), kind=jnp.bfloat16):
    level = steps_of(rng, shape, pieces, -0.22, 0.18) if pieces else 1.0
    drawn = jax.random.normal(rng, shape, jnp.float32) * spread * level
    return jnp.minimum(jnp.maximum(drawn, -limit), limit).astype(kind)


def setup_inputs(seed: int = 0) -> dict:
    streams_of = jax.random.split(jax.random.key(seed), 5)
    return {
        "noisy_qkv": draw_noisy_qkv(jax.random.fold_in(streams_of[4], 71), 0),
        "clean_cache": gaussian(streams_of[1], (N_SPAN, SPAN_TOK, 2, WIDTH), 1.0, 6.0, ((0, 8), (1, 32))),
        "span_ids": jax.random.permutation(streams_of[2], N_SPAN).astype(jnp.int32),
        "sign_bits": touch_ends((jax.random.randint(streams_of[3], (HD,), 0, 2) < 1).astype(jnp.int32), jax.random.fold_in(streams_of[3], 1), 0, 1),
    }


def hadamard_table(extent):
    row_index = lax.broadcasted_iota(jnp.int32, (extent, extent), 0)
    col_index = lax.broadcasted_iota(jnp.int32, (extent, extent), 1)
    parity = jnp.zeros((extent, extent), jnp.int32)
    for digit in range(extent.bit_length() - 1):
        parity = parity + row_index // 2 ** digit % 2 * (col_index // 2 ** digit % 2)
    return (1 - 2 * (parity % 2)).astype(jnp.float32)

def turn_back(stored, hadamard, sign_scale):
    return jnp.dot(stored.astype(jnp.float32), hadamard, precision=lax.Precision.HIGHEST) * sign_scale

def reference(noisy_qkv, clean_cache, span_ids, sign_bits):
    hadamard = hadamard_table(HD)
    sign_scale = (2 * sign_bits - 1).astype(jnp.float32) / math.sqrt(HD)
    score_scale = 1.0 / math.sqrt(HD)
    cached = clean_cache.reshape(N_SPAN, SPAN_TOK, 2, HEADS, HD)
    stored_keys = cached[:, :, 0]
    rotated_values = cached[:, :, 1]
    fresh = noisy_qkv.reshape(N_SPAN, SPAN_TOK, 3, HEADS, HD)
    group_list = jnp.arange(N_SPAN, dtype=jnp.int32)
    head_list = jnp.arange(HEADS, dtype=jnp.int32)

    def one_group(group_index):
        own_rows = lax.dynamic_index_in_dim(fresh, group_index, 0, keepdims=False)
        own_id = lax.dynamic_index_in_dim(span_ids, group_index, 0, keepdims=False)
        key_seen = jnp.repeat(span_ids < own_id, SPAN_TOK)

        def one_head(head_index):
            own_head = lax.dynamic_index_in_dim(own_rows, head_index, 2, keepdims=False)
            queries = own_head[:, 0]
            own_key = own_head[:, 1]
            own_value = own_head[:, 2]
            far_keys = lax.dynamic_index_in_dim(stored_keys, head_index, 2, keepdims=False).reshape(N_SPAN * SPAN_TOK, HD)
            far_values = lax.dynamic_index_in_dim(rotated_values, head_index, 2, keepdims=False).reshape(N_SPAN * SPAN_TOK, HD)
            turned_query = jnp.dot(queries.astype(jnp.float32) * sign_scale, hadamard, precision=lax.Precision.HIGHEST).astype(jnp.bfloat16)
            near_scores = jnp.dot(queries, own_key.T, preferred_element_type=jnp.float32) * score_scale
            far_scores = jnp.dot(turned_query, far_keys.T, preferred_element_type=jnp.float32) * score_scale
            far_scores = jnp.where(key_seen[None, :], far_scores, -jnp.inf)
            row_max = jnp.maximum(lax.optimization_barrier(jnp.max(near_scores, axis=1)), lax.optimization_barrier(jnp.max(far_scores, axis=1)))
            near_weights = jnp.exp(near_scores - row_max[:, None])
            far_weights = jnp.exp(far_scores - row_max[:, None])
            row_sum = lax.optimization_barrier(jnp.sum(near_weights, axis=1)) + lax.optimization_barrier(jnp.sum(far_weights, axis=1))
            near_part = jnp.dot(near_weights.astype(jnp.bfloat16), own_value, preferred_element_type=jnp.float32)
            far_rotated = jnp.dot(far_weights.astype(jnp.bfloat16), far_values, preferred_element_type=jnp.float32)
            far_part = turn_back(far_rotated, hadamard, sign_scale)
            return (near_part + far_part) / row_sum[:, None]
        per_head = lax.map(one_head, head_list)
        return jnp.transpose(per_head, (1, 0, 2)).reshape(SPAN_TOK, WIDTH).astype(jnp.bfloat16)
    return lax.map(one_group, group_list)
```

```python
import math

import jax
import jax.numpy as jnp
from jax import lax
from jax.experimental import pallas as pl
from jax.experimental.pallas import tpu as pltpu
from jax.sharding import PartitionSpec as P

HD = 128
ROW = 8
LOG2E_SCALE = math.log2(math.e) / math.sqrt(HD)
HIDDEN = -1e30
OFF = 1e30
F32 = jnp.float32
BF16 = jnp.bfloat16


def turn_matrix(sign_row):
    row = lax.broadcasted_iota(jnp.int32, (HD, HD), 0)
    col = lax.broadcasted_iota(jnp.int32, (HD, HD), 1)
    both = row & col
    parity = jnp.zeros((HD, HD), jnp.int32)
    for digit in range(HD.bit_length() - 1):
        parity = parity + ((both >> digit) & 1)
    entry = 1 - 2 * (parity & 1)
    return (entry * (2 * sign_row - 1)).astype(F32).astype(BF16)


def make_kernel(n_span, n_seq, tiles, x_size):
    ring = n_span // x_size
    unit = n_seq * tiles
    tokens = unit * ROW
    n_chunk = 4
    chunk = tokens // n_chunk
    own = n_span
    per_chunk = n_seq // n_chunk

    def kernel(
        sign_ref, id_ref, cache_ref, noisy_ref, out_ref,
        kv, qraw, sides, key_s, val_s, m_s, l_s, a_s, outbuf,
        in_send, in_recv, local_sem, ring_send, ring_recv, out_send, out_recv,
    ):
        span = lax.axis_index("span")
        seq = lax.axis_index("seq")
        x = span // ring
        y = span % ring
        x_other = (x + 1) % x_size
        up, down = (y + 1) % ring, (y + ring - 1) % ring
        partner = x_other * ring + y
        above, below = x * ring + up, x * ring + down
        far_above, far_below = x_other * ring + up, x_other * ring + down

        barrier = pltpu.get_barrier_semaphore()

        def greet(k, carry):
            t = lax.rem(seq + k, n_seq)
            pl.semaphore_signal(barrier, inc=1, device_id=(span, t))
            return carry

        lax.fori_loop(1, n_seq, greet, 0)
        for target in (partner, above, below):
            pl.semaphore_signal(barrier, inc=1, device_id=(target, seq))
        pl.semaphore_wait(barrier, n_seq - 1 + 3)

        mine = pl.ds(seq * tiles, tiles)

        def columns(t):
            return pl.ds(pl.multiple_of(t * HD, HD), HD)

        def scatter(src, dst, which):
            def send(k, carry):
                t = lax.rem(seq + k, n_seq)
                pltpu.make_async_remote_copy(
                    src_ref=src.at[:, :, columns(t)],
                    dst_ref=dst.at[mine],
                    send_sem=in_send.at[which],
                    recv_sem=in_recv.at[which],
                    device_id=(span, t),
                ).start()
                return carry

            lax.fori_loop(1, n_seq, send, 0)
            pltpu.make_async_copy(src.at[:, :, columns(seq)], dst.at[mine], in_recv.at[which]).start()

        def scattered(dst, which):
            whole = dst.at[pl.ds(0, unit)]
            pltpu.make_async_copy(whole, whole, in_recv.at[which]).wait()

        def unit_of(kind, j):
            return kv.at[kind, j, pl.ds(0, unit + 1 - kind)]

        def pass_on(kind, j, target, slot):
            pltpu.make_async_remote_copy(
                src_ref=unit_of(kind, j),
                dst_ref=unit_of(kind, j),
                send_sem=ring_send.at[slot],
                recv_sem=ring_recv.at[kind, j],
                device_id=(target, seq),
            ).start()

        def sent(kind, j, slot):
            whole = unit_of(kind, j)
            pltpu.make_async_copy(whole, whole, ring_send.at[slot]).wait()

        def arrived(kind, j):
            whole = unit_of(kind, j)
            pltpu.make_async_copy(whole, whole, ring_recv.at[kind, j]).wait()

        scatter(cache_ref.at[0], kv.at[0, span], 0)
        scatter(cache_ref.at[1], kv.at[1, span], 1)

        my_id = jnp.full((ROW, HD), id_ref[0], jnp.int32).astype(F32)
        kv[0, span, unit] = my_id.astype(BF16)
        kv[0, own, unit] = jnp.full((ROW, HD), -1.0, F32).astype(BF16)
        m_s[...] = jnp.full(m_s.shape, HIDDEN, F32)
        l_s[...] = jnp.zeros(l_s.shape, F32)
        a_s[...] = jnp.zeros(a_s.shape, F32)
        val_s[:, HD:] = jnp.ones((tokens, HD), BF16)
        turn = turn_matrix(sign_ref[...])

        scattered(kv.at[0, span], 0)
        pass_on(0, span, above, 0)
        pass_on(0, span, below, 1)
        pass_on(0, span, partner, 2)
        scatter(noisy_ref.at[0], qraw, 2)
        scattered(kv.at[1, span], 1)
        pass_on(1, span, above, 3)
        pass_on(1, span, below, 4)
        pass_on(1, span, partner, 5)
        scatter(noisy_ref.at[1], kv.at[0, own], 3)
        scatter(noisy_ref.at[2], kv.at[1, own], 4)
        arrived(0, partner)
        pass_on(0, partner, above, 6)
        pass_on(0, partner, below, 7)
        arrived(1, partner)
        pass_on(1, partner, above, 8)
        pass_on(1, partner, below, 9)
        arrived(0, below)
        pass_on(0, below, above, 10)
        arrived(1, above)
        pass_on(1, above, below, 11)

        scattered(qraw, 2)
        query = qraw[...].astype(F32).reshape(tokens, HD).astype(BF16)
        sides[1] = query
        sides[0] = (
            lax.dot_general(query, turn, (((1,), (1,)), ((), ())), preferred_element_type=F32)
            * (1.0 / math.sqrt(HD))
        ).astype(BF16)

        def dense(kind, j):
            return kv[kind, j, pl.ds(0, unit)].astype(F32).reshape(tokens, HD).astype(BF16)

        opposite = (y + 2) % ring
        order = (
            partner, above, below, far_above, own, far_below,
            x * ring + opposite, x_other * ring + opposite,
        )
        near_step = 4

        def step(i, carry):
            j = order[0]
            for place in range(1, len(order)):
                j = jnp.where(i == place, order[place], j)
            side = jnp.where(i == near_step, 1, 0)

            @pl.when(i == 2)
            def _():
                arrived(0, far_below)
                pass_on(0, far_below, above, 12)

            @pl.when(i == 3)
            def _():
                arrived(1, far_above)
                pass_on(1, far_above, below, 13)

            @pl.when(i == near_step)
            def _():
                scattered(kv.at[0, own], 3)
                scattered(kv.at[1, own], 4)

            @pl.when((i == 1) | (i == 3) | (i > 5))
            def _():
                arrived(0, j)

            @pl.when((i == 2) | (i > 4))
            def _():
                arrived(1, j)

            key_s[...] = dense(0, j)
            val_s[:, :HD] = dense(1, j)
            seen = (kv[0, j, unit].astype(F32) < my_id)[:1, :1]

            for c in range(n_chunk):
                rows = pl.ds(c * chunk, chunk)
                scores = lax.dot_general(
                    sides[side, rows], key_s[...], (((1,), (1,)), ((), ())),
                    preferred_element_type=F32,
                )
                top = jnp.max(scores, axis=1, keepdims=True) * LOG2E_SCALE
                top = jnp.where(seen, top, HIDDEN)
                old = m_s[side, rows][:, :1]
                new = jnp.maximum(old, top)
                weights = jnp.exp2(scores * LOG2E_SCALE - jnp.where(seen, new, OFF)).astype(BF16)
                factor = jnp.exp2(old - new)
                part = jnp.dot(weights, val_s[...], preferred_element_type=F32)
                l_s[side, rows] = l_s[side, rows] * factor + part[:, HD:]
                a_s[side, rows] = a_s[side, rows] * factor + part[:, :HD]
                m_s[side, rows] = jnp.broadcast_to(new, (chunk, HD))
            return carry

        lax.fori_loop(0, len(order), step, 0)

        def finish(k, carry):
            c = lax.rem(k + seq // per_chunk, n_chunk)
            rows = pl.ds(pl.multiple_of(c * chunk, chunk), chunk)
            best = jnp.maximum(m_s[0, rows], m_s[1, rows])
            far_factor = jnp.exp2(m_s[0, rows] - best)
            near_factor = jnp.exp2(m_s[1, rows] - best)
            far = a_s[0, rows]
            high = far.astype(BF16)
            low = (far - high.astype(F32)).astype(BF16)
            turned = (
                jnp.dot(high, turn, preferred_element_type=F32)
                + jnp.dot(low, turn, preferred_element_type=F32)
            ) * (1.0 / math.sqrt(HD))
            total = l_s[0, rows] * far_factor + l_s[1, rows] * near_factor
            result = (a_s[1, rows] * near_factor + turned * far_factor) / total
            outbuf[pl.ds(c * per_chunk * tiles, per_chunk * tiles)] = (
                result.reshape(per_chunk * tiles, ROW, HD).astype(BF16)
            )

            def give(u, inner):
                t = c * per_chunk + u
                piece = outbuf.at[pl.ds(t * tiles, tiles)]
                place = out_ref.at[:, :, columns(seq)]

                @pl.when(t != seq)
                def _():
                    pltpu.make_async_remote_copy(
                        src_ref=piece, dst_ref=place, send_sem=out_send, recv_sem=out_recv,
                        device_id=(span, t),
                    ).start()

                @pl.when(t == seq)
                def _():
                    pltpu.make_async_copy(piece, place, out_recv).start()

                return inner

            lax.fori_loop(0, per_chunk, give, 0)
            return carry

        lax.fori_loop(0, n_chunk, finish, 0)

        others = kv.at[0, 0, pl.ds(0, (n_seq - 1) * tiles)]
        for which in range(5):
            pltpu.make_async_copy(others, others, in_send.at[which]).wait()
        for slot, (kind, j) in enumerate(
            [(0, span)] * 3 + [(1, span)] * 3 + [(0, partner)] * 2 + [(1, partner)] * 2
            + [(0, below), (1, above), (0, far_below), (1, far_above)]
        ):
            sent(kind, j, slot)
        pltpu.make_async_copy(others, others, out_send).wait()
        pltpu.make_async_copy(outbuf, outbuf, out_recv).wait()

    return kernel


def per_device(noisy_qkv, clean_cache, span_ids, sign_bits):
    n_span, n_seq = lax.axis_size("span"), lax.axis_size("seq")
    _, rows, _, width = noisy_qkv.shape
    tiles = rows // ROW
    unit = n_seq * tiles
    tokens = unit * ROW
    noisy = jnp.transpose(noisy_qkv[0], (1, 0, 2)).reshape(3, tiles, ROW, width)
    cache = jnp.transpose(clean_cache[0], (1, 0, 2)).reshape(2, tiles, ROW, width)
    vmem, anywhere = pl.BlockSpec(memory_space=pltpu.VMEM), pl.BlockSpec(memory_space=pl.ANY)
    smem = pl.BlockSpec(memory_space=pltpu.SMEM)
    dma = pltpu.SemaphoreType.DMA
    out = pl.pallas_call(
        make_kernel(n_span, n_seq, tiles, 2),
        out_shape=jax.ShapeDtypeStruct((tiles, ROW, width), BF16),
        in_specs=[vmem, smem, anywhere, anywhere],
        out_specs=anywhere,
        scratch_shapes=[
            pltpu.VMEM((2, n_span + 1, unit + 1, ROW, HD), BF16),
            pltpu.VMEM((unit, ROW, HD), BF16),
            pltpu.VMEM((2, tokens, HD), BF16),
            pltpu.VMEM((tokens, HD), BF16),
            pltpu.VMEM((tokens, 2 * HD), BF16),
            pltpu.VMEM((2, tokens, HD), F32),
            pltpu.VMEM((2, tokens, HD), F32),
            pltpu.VMEM((2, tokens, HD), F32),
            pltpu.VMEM((unit, ROW, HD), BF16),
            dma((5,)), dma((5,)), dma, dma((14,)), dma((2, n_span)), dma, dma,
        ],
        compiler_params=pltpu.CompilerParams(
            collective_id=0, has_side_effects=True, vmem_limit_bytes=50 * 2**20
        ),
        cost_estimate=pl.CostEstimate(
            flops=8 * 4 * tokens * tokens * HD, bytes_accessed=2 * 2**20,
            transcendentals=8 * tokens * tokens,
        ),
        name="span_attention",
    )(sign_bits.reshape(1, HD), span_ids, cache, noisy)
    return out.reshape(1, rows, width)


def solution(mesh):
    placed = (P("span", "seq", None, None), P("span", "seq", None, None), P("span"), P())
    return jax.shard_map(
        per_device, mesh=mesh, in_specs=placed, out_specs=P("span", "seq", None), check_vma=False
    )
```

```python
import math

import jax
import jax.numpy as jnp
from jax import lax
from jax.experimental import pallas as pl
from jax.experimental.pallas import tpu as pltpu
from jax.sharding import PartitionSpec as P

HD = 128
ROW = 8
X_SIZE = 2
N_CHUNK = 4
SPREAD = 64
LOG2E_SCALE = math.log2(math.e) / math.sqrt(HD)
HIDDEN = -1e30
OFF = 1e30
F32 = jnp.float32
BF16 = jnp.bfloat16


def turn_matrix(sign_row):
    row = lax.broadcasted_iota(jnp.int32, (HD, HD), 0)
    col = lax.broadcasted_iota(jnp.int32, (HD, HD), 1)
    both = row & col
    parity = jnp.zeros((HD, HD), jnp.int32)
    for digit in range(HD.bit_length() - 1):
        parity = parity + ((both >> digit) & 1)
    entry = 1 - 2 * (parity & 1)
    return (entry * (2 * sign_row - 1)).astype(F32).astype(BF16)


def make_kernel(n_span, n_seq, tiles, x_size):
    ring = n_span // x_size
    line = n_seq // 4
    unit = n_seq * tiles
    tokens = unit * ROW
    half_unit, half = unit // 2, tokens // 2
    n_chunk = N_CHUNK
    chunk = tokens // n_chunk
    near = ring
    per_chunk = n_seq // n_chunk
    id_rows = pl.ds(tokens, 2 * ROW)

    def kernel(
        sign_ref, id_ref, cache_ref, noisy_ref, out_ref,
        kv, qraw, sides, key_s, val_s, m_s, l_s, a_s, part_out, part_in, stat_out, stat_in, outbuf,
        in_send, in_recv, ring_send, ring_recv, x_send, x_recv, out_send, out_recv,
    ):
        span = lax.axis_index("span")
        seq = lax.axis_index("seq")
        x = span // ring
        y = span % ring
        above, below = (y + 1) % ring, (y + ring - 1) % ring
        opposite = (y + 2) % ring
        partner = ((x + 1) % x_size) * ring + y
        lane, plane = seq % 2, seq // (n_seq // 2)
        spot = seq // 2 % line
        corner = plane * 2 + lane

        def seat(distance, place):
            return place // 2 * 2 * line + lax.rem(spot + distance + line, line) * 2 + place % 2

        barrier = pltpu.get_barrier_semaphore()

        def greet(k, carry):
            pl.semaphore_signal(barrier, inc=1, device_id=(span, lax.rem(seq + k, n_seq)))
            return carry

        lax.fori_loop(1, n_seq, greet, 0)
        for target in (partner, x * ring + above, x * ring + below):
            pl.semaphore_signal(barrier, inc=1, device_id=(target, seq))
        pl.semaphore_wait(barrier, n_seq - 1 + 3)

        def columns(t):
            return pl.ds(pl.multiple_of(t * HD, HD), HD)

        def slab(first, slot):
            return pl.ds(first + slot * tiles, tiles)

        two = jnp.where(lane == 1, 2, -2)
        routes = (
            ((0, 0), (1, 8), (-1, 4), (two, 12)),
            ((4, 28), (3, 24), (-3, 20), (-two, 16)),
        )

        def scatter(src, dst, first, which, group):
            for distance, base in routes[group]:
                here = dst.at[slab(first, base + corner)]

                def send(p, carry, distance=distance, here=here):
                    t = seat(distance, lax.rem(corner + p, 4))
                    pltpu.make_async_remote_copy(
                        src_ref=src.at[:, :, columns(t)],
                        dst_ref=here,
                        send_sem=in_send.at[which, group],
                        recv_sem=in_recv.at[which, group],
                        device_id=(span, t),
                    ).start()
                    return carry

                if group == 0 and base == 0:
                    lax.fori_loop(1, 4, send, 0)
                    pltpu.make_async_copy(
                        src.at[:, :, columns(seq)], here, in_recv.at[which, group]
                    ).start()
                else:
                    lax.fori_loop(0, 4, send, 0)

        def scattered(dst, first, which, group):
            whole = dst.at[pl.ds(first + group * half_unit, half_unit)]
            pltpu.make_async_copy(whole, whole, in_recv.at[which, group]).wait()

        def unit_of(kind, j, group):
            if group == 0:
                return kv.at[kind, j, pl.ds(kind, half_unit + 1 - kind)]
            return kv.at[kind, j, pl.ds(1 + half_unit, half_unit)]

        ring_sent = []

        def pass_on(kind, j, group, target):
            pltpu.make_async_remote_copy(
                src_ref=unit_of(kind, j, group),
                dst_ref=unit_of(kind, j, group),
                send_sem=ring_send.at[len(ring_sent)],
                recv_sem=ring_recv.at[kind, j, group],
                device_id=(x * ring + target, seq),
            ).start()
            ring_sent.append((kind, j, group))

        def arrived(kind, j, group):
            whole = unit_of(kind, j, group)
            pltpu.make_async_copy(whole, whole, ring_recv.at[kind, j, group]).wait()

        def cross(src, dst, slot):
            return pltpu.make_async_remote_copy(
                src_ref=src, dst_ref=dst, send_sem=x_send.at[slot], recv_sem=x_recv.at[slot],
                device_id=(partner, seq),
            )

        queries_across = cross(sides.at[0], sides.at[2], 0)

        def rows_of(c):
            return pl.ds(c * chunk, chunk)

        parts_across = [
            cross(part_out.at[rows_of(c)], part_in.at[rows_of(c)], 1 + c) for c in range(n_chunk)
        ]
        stats_across = [
            cross(stat_out.at[c], stat_in.at[c], 1 + n_chunk + c) for c in range(n_chunk)
        ]

        scatter(cache_ref.at[0], kv.at[0, y], 1, 0, 0)
        scatter(cache_ref.at[1], kv.at[1, y], 1, 1, 0)
        scatter(noisy_ref.at[0], qraw, 0, 2, 0)
        scatter(noisy_ref.at[0], qraw, 0, 2, 1)

        my_id = jnp.full((2 * ROW, HD), id_ref[0], jnp.int32).astype(F32).astype(BF16)
        kv[0, y, 0] = my_id[:ROW]
        sides[0, id_rows] = my_id
        m_s[...] = jnp.full(m_s.shape, HIDDEN, F32)
        l_s[...] = jnp.zeros(l_s.shape, F32)
        a_s[...] = jnp.zeros(a_s.shape, F32)
        for j in range(ring + 1):
            val_s[j, :, HD:] = jnp.ones((tokens, HD), BF16)
        stat_out[...] = jnp.zeros(stat_out.shape, F32)
        turn = turn_matrix(sign_ref[...])

        scattered(kv.at[0, y], 1, 0, 0)
        pass_on(0, y, 0, above)
        pass_on(0, y, 0, below)
        scattered(kv.at[1, y], 1, 1, 0)
        pass_on(1, y, 0, above)
        pass_on(1, y, 0, below)
        scatter(cache_ref.at[0], kv.at[0, y], 1, 0, 1)
        arrived(0, below, 0)
        pass_on(0, below, 0, above)
        arrived(1, above, 0)
        pass_on(1, above, 0, below)
        scattered(qraw, 0, 2, 0)
        scattered(qraw, 0, 2, 1)
        query = qraw[...].astype(F32).reshape(tokens, HD).astype(BF16)
        sides[0, pl.ds(0, tokens)] = (
            lax.dot_general(query, turn, (((1,), (1,)), ((), ())), preferred_element_type=F32)
            * (1.0 / math.sqrt(HD))
        ).astype(BF16)
        queries_across.start()
        sides[1, pl.ds(0, tokens)] = query
        scatter(cache_ref.at[1], kv.at[1, y], 1, 1, 1)

        plan = (
            (0, above, 0), (0, below, 0), (0, opposite, 0),
            (2, y, 0), (2, above, 0), (2, below, 0), (2, opposite, 0),
            (2, y, 1), (2, above, 1), (2, below, 1), (2, opposite, 1),
            (0, above, 1), (0, below, 1), (0, opposite, 1),
        )

        def pick(i, field):
            got = plan[0][field]
            for place in range(1, len(plan)):
                got = jnp.where(i == place, plan[place][field], got)
            return got

        diagonal = lax.broadcasted_iota(jnp.int32, (SPREAD, HD), 0) == lax.broadcasted_iota(
            jnp.int32, (SPREAD, HD), 1
        )

        def loosen(j, group, size, count):
            rows = pl.ds(pl.multiple_of(group * half, half), size)
            for kind, dst in ((0, key_s), (1, val_s)):
                dst[j, rows, :HD] = (
                    kv[kind, j, pl.ds(1 + group * half_unit, count)]
                    .astype(F32).reshape(size, HD).astype(BF16)
                )

        def score(side, rows, keys):
            return lax.dot_general(
                sides[side, rows], keys, (((1,), (1,)), ((), ())), preferred_element_type=F32
            )

        def absorb(state, side, j, group, order, after):
            seen = (kv[0, j, 0].astype(F32) < sides[side, id_rows].astype(F32)[:ROW])[:1, :1]
            here = pl.ds(pl.multiple_of(group * half, half), half)
            ahead = score(side, rows_of(order[0]), key_s[j, here])
            for place, c in enumerate(order):
                rows = rows_of(c)
                scores = ahead
                if place + 1 < n_chunk:
                    ahead = score(side, rows_of(order[place + 1]), key_s[j, here])
                top = jnp.max(scores, axis=1, keepdims=True) * LOG2E_SCALE
                top = jnp.where(seen, top, HIDDEN)
                old = m_s[state, rows][:, :1]
                new = jnp.maximum(old, top)
                weights = jnp.exp2(scores * LOG2E_SCALE - jnp.where(seen, new, OFF)).astype(BF16)
                factor = jnp.exp2(old - new)
                part = jnp.dot(weights, val_s[j, here], preferred_element_type=F32)
                l_s[state, rows] = l_s[state, rows] * factor + part[:, HD:]
                a_s[state, rows] = a_s[state, rows] * factor + part[:, :HD]
                m_s[state, rows] = jnp.broadcast_to(new, (chunk, HD))
                after(c)

        def step(i, carry):
            side, j, group = pick(i, 0), pick(i, 1), pick(i, 2)

            @pl.when(i == 0)
            def _():
                arrived(0, above, 0)

            @pl.when(i == 1)
            def _():
                arrived(1, below, 0)

            @pl.when(i == 2)
            def _():
                arrived(0, opposite, 0)
                arrived(1, opposite, 0)

            @pl.when(i == 3)
            def _():
                scattered(kv.at[0, y], 1, 0, 1)
                pass_on(0, y, 1, above)
                pass_on(0, y, 1, below)
                for group in range(2):
                    scatter(noisy_ref.at[1], kv.at[0, near], 1, 3, group)
                queries_across.wait_recv()

            @pl.when(i == 6)
            def _():
                scattered(kv.at[1, y], 1, 1, 1)
                pass_on(1, y, 1, above)
                pass_on(1, y, 1, below)
                for group in range(2):
                    scatter(noisy_ref.at[2], kv.at[1, near], 1, 4, group)

            @pl.when(i == 7)
            def _():
                arrived(0, below, 1)
                pass_on(0, below, 1, above)

            @pl.when(i == 8)
            def _():
                arrived(1, above, 1)
                pass_on(1, above, 1, below)
                arrived(0, above, 1)

            @pl.when(i == 9)
            def _():
                arrived(1, below, 1)

            @pl.when((i < 4) | (i > 6))
            def _():
                loosen(j, group, half, half_unit)

            absorb(side // 2, side, j, group, tuple(range(n_chunk)), lambda c: None)
            return carry

        lax.fori_loop(0, 10, step, 0)

        arrived(0, opposite, 1)
        arrived(1, opposite, 1)
        loosen(opposite, 1, half, half_unit)

        def give_part(c):
            part_out[rows_of(c)] = a_s[1, rows_of(c)].astype(BF16)
            for b in range(chunk // SPREAD):
                rows = pl.ds(c * chunk + b * SPREAD, SPREAD)
                for place, stat in ((0, m_s), (ROW, l_s)):
                    stat_out[c, pl.ds(place + b, 1)] = jnp.sum(
                        jnp.where(diagonal, stat[1, rows], 0.0), axis=0, keepdims=True
                    )
            parts_across[c].start()
            stats_across[c].start()

        backward = tuple(reversed(range(n_chunk)))
        absorb(1, 2, opposite, 1, backward, give_part)

        def own_step(i, carry):
            absorb(0, 0, pick(i, 1), 1, tuple(range(n_chunk)), lambda c: None)
            return carry

        lax.fori_loop(11, len(plan), own_step, 0)

        for which in (3, 4):
            for group in range(2):
                scattered(kv.at[which - 3, near], 1, which, group)
        loosen(near, 0, tokens, unit)
        place = out_ref.at[:, :, columns(seq)]

        def give(slot, t):
            pltpu.make_async_remote_copy(
                src_ref=outbuf.at[slab(0, slot)], dst_ref=place,
                send_sem=out_send, recv_sem=out_recv, device_id=(span, t),
            ).start()

        back = ((0, 0), (1, 1), (-1, -1), (2, -2), (-2, 2), (3, 3), (-3, -3), (4, 4))
        ahead = score(1, pl.ds((n_chunk - 1) * chunk, chunk), key_s[near])
        for c in backward:
            rows = rows_of(c)
            scores = ahead
            if c > 0:
                ahead = score(1, pl.ds((c - 1) * chunk, chunk), key_s[near])
            top = jnp.max(scores, axis=1, keepdims=True) * LOG2E_SCALE
            weights = jnp.exp2(scores * LOG2E_SCALE - top).astype(BF16)
            part = jnp.dot(weights, val_s[near], preferred_element_type=F32)
            parts_across[c].wait_recv()
            stats_across[c].wait_recv()
            for b in range(chunk // SPREAD):
                some = pl.ds(c * chunk + b * SPREAD, SPREAD)
                for start, stat in ((0, m_s), (ROW, l_s)):
                    spread = jnp.broadcast_to(stat_in[c, pl.ds(start + b, 1)], (SPREAD, HD))
                    stat[1, some] = jnp.broadcast_to(
                        jnp.sum(jnp.where(diagonal, spread, 0.0), axis=1, keepdims=True),
                        (SPREAD, HD),
                    )
            best = jnp.maximum(jnp.maximum(m_s[0, rows], m_s[1, rows]), top)
            far_factor = jnp.exp2(m_s[0, rows] - best)
            near_factor = jnp.exp2(top - best)
            across_factor = jnp.exp2(m_s[1, rows] - best)
            far = a_s[0, rows] * far_factor + part_in[rows].astype(F32) * across_factor
            high = far.astype(BF16)
            low = (far - high.astype(F32)).astype(BF16)
            turned = (
                jnp.dot(high, turn, preferred_element_type=F32)
                + jnp.dot(low, turn, preferred_element_type=F32)
            ) * (1.0 / math.sqrt(HD))
            total = (
                l_s[0, rows] * far_factor + part[:, HD:] * near_factor + l_s[1, rows] * across_factor
            )
            result = (part[:, :HD] * near_factor + turned) / total
            outbuf[pl.ds(c * per_chunk * tiles, per_chunk * tiles)] = (
                result.reshape(per_chunk * tiles, ROW, HD).astype(BF16)
            )
            for g in reversed(range(2 * c, 2 * c + 2)):
                for p in range(4):
                    if g > 0:
                        give(4 * g + p, seat(back[g][p % 2], p))
                    elif p > 0:
                        other = lax.rem(corner + p, 4)
                        give(other, seat(0, other))
        own_copy = pltpu.make_async_copy(outbuf.at[slab(0, corner)], place, out_recv)
        own_copy.start()

        def drained(count, sem):
            some = outbuf.at[pl.ds(0, count * tiles)]
            pltpu.make_async_copy(some, some, sem).wait()

        for which in range(5):
            drained(n_seq // 2 - 1, in_send.at[which, 0])
            drained(n_seq // 2, in_send.at[which, 1])
        for slot, (kind, j, group) in enumerate(ring_sent):
            whole = unit_of(kind, j, group)
            pltpu.make_async_copy(whole, whole, ring_send.at[slot]).wait()
        for copy in [queries_across] + parts_across + stats_across:
            copy.wait_send()
        drained(n_seq - 1, out_send)
        drained(n_seq, out_recv)

    return kernel


def per_device(noisy_qkv, clean_cache, span_ids, sign_bits):
    n_span, n_seq = lax.axis_size("span"), lax.axis_size("seq")
    _, rows, _, width = noisy_qkv.shape
    tiles = rows // ROW
    unit = n_seq * tiles
    tokens = unit * ROW
    ring = n_span // X_SIZE
    noisy = jnp.transpose(noisy_qkv[0], (1, 0, 2)).reshape(3, tiles, ROW, width)
    cache = jnp.transpose(clean_cache[0], (1, 0, 2)).reshape(2, tiles, ROW, width)
    vmem, anywhere = pl.BlockSpec(memory_space=pltpu.VMEM), pl.BlockSpec(memory_space=pl.ANY)
    smem = pl.BlockSpec(memory_space=pltpu.SMEM)
    dma = pltpu.SemaphoreType.DMA
    out = pl.pallas_call(
        make_kernel(n_span, n_seq, tiles, X_SIZE),
        out_shape=jax.ShapeDtypeStruct((tiles, ROW, width), BF16),
        in_specs=[vmem, smem, anywhere, anywhere],
        out_specs=anywhere,
        scratch_shapes=[
            pltpu.VMEM((2, ring + 1, unit + 1, ROW, HD), BF16),
            pltpu.VMEM((unit, ROW, HD), BF16),
            pltpu.VMEM((3, tokens + 2 * ROW, HD), BF16),
            pltpu.VMEM((ring + 1, tokens, HD), BF16),
            pltpu.VMEM((ring + 1, tokens, 2 * HD), BF16),
            pltpu.VMEM((2, tokens, HD), F32),
            pltpu.VMEM((2, tokens, HD), F32),
            pltpu.VMEM((2, tokens, HD), F32),
            pltpu.VMEM((tokens, HD), BF16),
            pltpu.VMEM((tokens, HD), BF16),
            pltpu.VMEM((N_CHUNK, 2 * ROW, HD), F32),
            pltpu.VMEM((N_CHUNK, 2 * ROW, HD), F32),
            pltpu.VMEM((unit, ROW, HD), BF16),
            dma((5, 2)), dma((5, 2)), dma((12,)), dma((2, ring, 2)),
            dma((2 * N_CHUNK + 1,)), dma((2 * N_CHUNK + 1,)), dma, dma,
        ],
        compiler_params=pltpu.CompilerParams(
            collective_id=0, has_side_effects=True, vmem_limit_bytes=50 * 2**20
        ),
        cost_estimate=pl.CostEstimate(
            flops=8 * 4 * tokens * tokens * HD, bytes_accessed=2 * 2**20,
            transcendentals=8 * tokens * tokens,
        ),
        name="span_attention",
    )(sign_bits.reshape(1, HD), span_ids, cache, noisy)
    return out.reshape(1, rows, width)


def solution(mesh):
    placed = (P("span", "seq", None, None), P("span", "seq", None, None), P("span"), P())
    return jax.shard_map(
        per_device, mesh=mesh, in_specs=placed, out_specs=P("span", "seq", None), check_vma=False
    )
```

```python
import math

import jax
import jax.numpy as jnp
from jax import lax
from jax.experimental import pallas as pl
from jax.experimental.pallas import tpu as pltpu
from jax.sharding import PartitionSpec as P

HD = 128
ROW = 8
X_SIZE = 2
N_CHUNK = 4
SPREAD = 64
LOG2E_SCALE = math.log2(math.e) / math.sqrt(HD)
HIDDEN = -1e30
OFF = 1e30
F32 = jnp.float32
BF16 = jnp.bfloat16


def turn_matrix(sign_row):
    row = lax.broadcasted_iota(jnp.int32, (HD, HD), 0)
    col = lax.broadcasted_iota(jnp.int32, (HD, HD), 1)
    both = row & col
    parity = jnp.zeros((HD, HD), jnp.int32)
    for digit in range(HD.bit_length() - 1):
        parity = parity + ((both >> digit) & 1)
    entry = 1 - 2 * (parity & 1)
    return (entry * (2 * sign_row - 1)).astype(F32).astype(BF16)


def make_kernel(n_span, n_seq, tiles, x_size):
    ring = n_span // x_size
    line = n_seq // 4
    unit = n_seq * tiles
    tokens = unit * ROW
    half_unit, half = unit // 2, tokens // 2
    n_chunk = N_CHUNK
    chunk = tokens // n_chunk
    near = ring
    per_chunk = n_seq // n_chunk
    id_rows = pl.ds(tokens, 2 * ROW)

    def kernel(
        sign_ref, id_ref, cache_ref, noisy_ref, out_ref,
        kv, qraw, sides, key_s, val_s, m_s, l_s, a_s, part_out, part_in, stat_out, stat_in, outbuf,
        in_send, in_recv, ring_send, ring_recv, x_send, x_recv, out_send, out_recv,
    ):
        span = lax.axis_index("span")
        seq = lax.axis_index("seq")
        x = span // ring
        y = span % ring
        above, below = (y + 1) % ring, (y + ring - 1) % ring
        opposite = (y + 2) % ring
        partner = ((x + 1) % x_size) * ring + y
        lane, plane = seq % 2, seq // (n_seq // 2)
        spot = seq // 2 % line
        corner = plane * 2 + lane

        def seat(distance, place):
            return place // 2 * 2 * line + lax.rem(spot + distance + line, line) * 2 + place % 2

        barrier = pltpu.get_barrier_semaphore()

        def greet(k, carry):
            pl.semaphore_signal(barrier, inc=1, device_id=(span, lax.rem(seq + k, n_seq)))
            return carry

        lax.fori_loop(1, n_seq, greet, 0)
        for target in (partner, x * ring + above, x * ring + below):
            pl.semaphore_signal(barrier, inc=1, device_id=(target, seq))
        pl.semaphore_wait(barrier, n_seq - 1 + 3)

        def columns(t):
            return pl.ds(pl.multiple_of(t * HD, HD), HD)

        def slab(first, slot):
            return pl.ds(first + slot * tiles, tiles)

        two = jnp.where(lane == 1, 2, -2)
        routes = (
            ((0, 0), (1, 8), (-1, 4), (two, 12)),
            ((4, 28), (3, 24), (-3, 20), (-two, 16)),
        )

        def scatter(src, dst, first, which, group):
            for distance, base in routes[group]:
                here = dst.at[slab(first, base + corner)]

                def send(p, carry, distance=distance, here=here):
                    t = seat(distance, lax.rem(corner + p, 4))
                    pltpu.make_async_remote_copy(
                        src_ref=src.at[:, :, columns(t)],
                        dst_ref=here,
                        send_sem=in_send.at[which, group],
                        recv_sem=in_recv.at[which, group],
                        device_id=(span, t),
                    ).start()
                    return carry

                if group == 0 and base == 0:
                    lax.fori_loop(1, 4, send, 0)
                    pltpu.make_async_copy(
                        src.at[:, :, columns(seq)], here, in_recv.at[which, group]
                    ).start()
                else:
                    lax.fori_loop(0, 4, send, 0)

        def scattered(dst, first, which, group):
            whole = dst.at[pl.ds(first + group * half_unit, half_unit)]
            pltpu.make_async_copy(whole, whole, in_recv.at[which, group]).wait()

        def unit_of(kind, j, group):
            if group == 0:
                return kv.at[kind, j, pl.ds(kind, half_unit + 1 - kind)]
            return kv.at[kind, j, pl.ds(1 + half_unit, half_unit)]

        ring_sent = []

        def pass_on(kind, j, group, target):
            pltpu.make_async_remote_copy(
                src_ref=unit_of(kind, j, group),
                dst_ref=unit_of(kind, j, group),
                send_sem=ring_send.at[len(ring_sent)],
                recv_sem=ring_recv.at[kind, j, group],
                device_id=(x * ring + target, seq),
            ).start()
            ring_sent.append((kind, j, group))

        def arrived(kind, j, group):
            whole = unit_of(kind, j, group)
            pltpu.make_async_copy(whole, whole, ring_recv.at[kind, j, group]).wait()

        def cross(src, dst, slot):
            return pltpu.make_async_remote_copy(
                src_ref=src, dst_ref=dst, send_sem=x_send.at[slot], recv_sem=x_recv.at[slot],
                device_id=(partner, seq),
            )

        queries_across = cross(sides.at[0], sides.at[2], 0)

        def rows_of(c):
            return pl.ds(c * chunk, chunk)

        parts_across = [
            cross(part_out.at[rows_of(c)], part_in.at[rows_of(c)], 1 + c) for c in range(n_chunk)
        ]
        stats_across = [
            cross(stat_out.at[c], stat_in.at[c], 1 + n_chunk + c) for c in range(n_chunk)
        ]

        scatter(cache_ref.at[0], kv.at[0, y], 1, 0, 0)
        scatter(cache_ref.at[1], kv.at[1, y], 1, 1, 0)
        scatter(noisy_ref.at[0], qraw, 0, 2, 0)
        scatter(noisy_ref.at[0], qraw, 0, 2, 1)

        my_id = jnp.full((2 * ROW, HD), id_ref[0], jnp.int32).astype(F32).astype(BF16)
        kv[0, y, 0] = my_id[:ROW]
        sides[0, id_rows] = my_id
        m_s[...] = jnp.full(m_s.shape, HIDDEN, F32)
        l_s[...] = jnp.zeros(l_s.shape, F32)
        a_s[...] = jnp.zeros(a_s.shape, F32)
        for j in range(ring + 1):
            val_s[j, :, HD:] = jnp.ones((tokens, HD), BF16)
        stat_out[...] = jnp.zeros(stat_out.shape, F32)
        turn = turn_matrix(sign_ref[...])

        scattered(kv.at[0, y], 1, 0, 0)
        pass_on(0, y, 0, above)
        pass_on(0, y, 0, below)
        scattered(kv.at[1, y], 1, 1, 0)
        pass_on(1, y, 0, above)
        pass_on(1, y, 0, below)
        scatter(cache_ref.at[0], kv.at[0, y], 1, 0, 1)
        arrived(0, below, 0)
        pass_on(0, below, 0, above)
        arrived(1, above, 0)
        pass_on(1, above, 0, below)
        scattered(qraw, 0, 2, 0)
        scattered(qraw, 0, 2, 1)
        query = qraw[...].astype(F32).reshape(tokens, HD).astype(BF16)
        sides[0, pl.ds(0, tokens)] = (
            lax.dot_general(query, turn, (((1,), (1,)), ((), ())), preferred_element_type=F32)
            * (1.0 / math.sqrt(HD))
        ).astype(BF16)
        queries_across.start()
        sides[1, pl.ds(0, tokens)] = query
        scatter(cache_ref.at[1], kv.at[1, y], 1, 1, 1)

        plan = (
            (0, above, 0), (0, below, 0), (0, opposite, 0),
            (2, y, 0), (2, above, 0), (2, below, 0), (2, opposite, 0),
            (2, y, 1), (2, above, 1), (2, below, 1), (2, opposite, 1),
            (0, above, 1), (0, below, 1), (0, opposite, 1),
        )

        def pick(i, field):
            got = plan[0][field]
            for place in range(1, len(plan)):
                got = jnp.where(i == place, plan[place][field], got)
            return got

        diagonal = lax.broadcasted_iota(jnp.int32, (SPREAD, HD), 0) == lax.broadcasted_iota(
            jnp.int32, (SPREAD, HD), 1
        )

        def loosen(j, group, size, count):
            rows = pl.ds(pl.multiple_of(group * half, half), size)
            for kind, dst in ((0, key_s), (1, val_s)):
                dst[j, rows, :HD] = (
                    kv[kind, j, pl.ds(1 + group * half_unit, count)]
                    .astype(F32).reshape(size, HD).astype(BF16)
                )

        def score(side, rows, keys):
            return lax.dot_general(
                sides[side, rows], keys, (((1,), (1,)), ((), ())), preferred_element_type=F32
            )

        def absorb(state, side, j, group, order, after):
            seen = (kv[0, j, 0].astype(F32) < sides[side, id_rows].astype(F32)[:ROW])[:1, :1]
            here = pl.ds(pl.multiple_of(group * half, half), half)
            ahead = score(side, rows_of(order[0]), key_s[j, here])
            for place, c in enumerate(order):
                rows = rows_of(c)
                scores = ahead
                if place + 1 < n_chunk:
                    ahead = score(side, rows_of(order[place + 1]), key_s[j, here])
                top = jnp.max(scores, axis=1, keepdims=True) * LOG2E_SCALE
                top = jnp.where(seen, top, HIDDEN)
                old = m_s[state, rows][:, :1]
                new = jnp.maximum(old, top)
                weights = jnp.exp2(scores * LOG2E_SCALE - jnp.where(seen, new, OFF)).astype(BF16)
                factor = jnp.exp2(old - new)
                part = jnp.dot(weights, val_s[j, here], preferred_element_type=F32)
                l_s[state, rows] = l_s[state, rows] * factor + part[:, HD:]
                a_s[state, rows] = a_s[state, rows] * factor + part[:, :HD]
                m_s[state, rows] = jnp.broadcast_to(new, (chunk, HD))
                after(c)

        def step(i, carry):
            side, j, group = pick(i, 0), pick(i, 1), pick(i, 2)

            @pl.when(i == 0)
            def _():
                arrived(0, above, 0)

            @pl.when(i == 1)
            def _():
                arrived(1, below, 0)

            @pl.when(i == 2)
            def _():
                arrived(0, opposite, 0)
                arrived(1, opposite, 0)

            @pl.when(i == 3)
            def _():
                for kind in range(2):
                    scattered(kv.at[kind, y], 1, kind, 1)
                    pass_on(kind, y, 1, above)
                    pass_on(kind, y, 1, below)
                for group in range(2):
                    scatter(noisy_ref.at[1], kv.at[0, near], 1, 3, group)
                queries_across.wait_recv()

            @pl.when(i == 4)
            def _():
                arrived(0, below, 1)
                pass_on(0, below, 1, above)

            @pl.when(i == 6)
            def _():
                arrived(1, above, 1)
                pass_on(1, above, 1, below)

            @pl.when(i == 7)
            def _():
                for group in range(2):
                    scatter(noisy_ref.at[2], kv.at[1, near], 1, 4, group)

            @pl.when(i == 8)
            def _():
                arrived(0, above, 1)

            @pl.when(i == 9)
            def _():
                arrived(1, below, 1)

            @pl.when((i < 4) | (i > 6))
            def _():
                loosen(j, group, half, half_unit)

            absorb(side // 2, side, j, group, tuple(range(n_chunk)), lambda c: None)
            return carry

        lax.fori_loop(0, 10, step, 0)

        arrived(0, opposite, 1)
        arrived(1, opposite, 1)
        loosen(opposite, 1, half, half_unit)

        backward = tuple(reversed(range(n_chunk)))

        def send_part(c):
            parts_across[c].start()
            stats_across[c].start()

        def give_part(c):
            part_out[rows_of(c)] = a_s[1, rows_of(c)].astype(BF16)
            for b in range(chunk // SPREAD):
                rows = pl.ds(c * chunk + b * SPREAD, SPREAD)
                for place, stat in ((0, m_s), (ROW, l_s)):
                    stat_out[c, pl.ds(place + b, 1)] = jnp.sum(
                        jnp.where(diagonal, stat[1, rows], 0.0), axis=0, keepdims=True
                    )
            if c == backward[0]:
                send_part(c)
            if c == backward[-1]:
                send_part(backward[1])

        absorb(1, 2, opposite, 1, backward, give_part)

        def own_step(i, carry):
            for place in range(2, n_chunk):

                @pl.when(i == 10 + place)
                def _(place=place):
                    send_part(backward[place])

            absorb(0, 0, pick(i, 1), 1, tuple(range(n_chunk)), lambda c: None)
            return carry

        lax.fori_loop(11, len(plan), own_step, 0)

        for which in (3, 4):
            for group in range(2):
                scattered(kv.at[which - 3, near], 1, which, group)
        loosen(near, 0, tokens, unit)
        place = out_ref.at[:, :, columns(seq)]

        def give(slot, t):
            pltpu.make_async_remote_copy(
                src_ref=outbuf.at[slab(0, slot)], dst_ref=place,
                send_sem=out_send, recv_sem=out_recv, device_id=(span, t),
            ).start()

        back = ((0, 0), (1, 1), (-1, -1), (2, -2), (-2, 2), (3, 3), (-3, -3), (4, 4))
        ahead = score(1, pl.ds((n_chunk - 1) * chunk, chunk), key_s[near])
        for c in backward:
            rows = rows_of(c)
            scores = ahead
            if c > 0:
                ahead = score(1, pl.ds((c - 1) * chunk, chunk), key_s[near])
            top = jnp.max(scores, axis=1, keepdims=True) * LOG2E_SCALE
            weights = jnp.exp2(scores * LOG2E_SCALE - top).astype(BF16)
            part = jnp.dot(weights, val_s[near], preferred_element_type=F32)
            parts_across[c].wait_recv()
            stats_across[c].wait_recv()
            for b in range(chunk // SPREAD):
                some = pl.ds(c * chunk + b * SPREAD, SPREAD)
                for start, stat in ((0, m_s), (ROW, l_s)):
                    spread = jnp.broadcast_to(stat_in[c, pl.ds(start + b, 1)], (SPREAD, HD))
                    stat[1, some] = jnp.broadcast_to(
                        jnp.sum(jnp.where(diagonal, spread, 0.0), axis=1, keepdims=True),
                        (SPREAD, HD),
                    )
            best = jnp.maximum(jnp.maximum(m_s[0, rows], m_s[1, rows]), top)
            far_factor = jnp.exp2(m_s[0, rows] - best)
            near_factor = jnp.exp2(top - best)
            across_factor = jnp.exp2(m_s[1, rows] - best)
            far = a_s[0, rows] * far_factor + part_in[rows].astype(F32) * across_factor
            high = far.astype(BF16)
            low = (far - high.astype(F32)).astype(BF16)
            turned = (
                jnp.dot(high, turn, preferred_element_type=F32)
                + jnp.dot(low, turn, preferred_element_type=F32)
            ) * (1.0 / math.sqrt(HD))
            total = (
                l_s[0, rows] * far_factor + part[:, HD:] * near_factor + l_s[1, rows] * across_factor
            )
            result = (part[:, :HD] * near_factor + turned) / total
            outbuf[pl.ds(c * per_chunk * tiles, per_chunk * tiles)] = (
                result.reshape(per_chunk * tiles, ROW, HD).astype(BF16)
            )
            for g in reversed(range(2 * c, 2 * c + 2)):
                for p in range(4):
                    if g > 0:
                        give(4 * g + p, seat(back[g][p % 2], p))
                    elif p > 0:
                        other = lax.rem(corner + p, 4)
                        give(other, seat(0, other))
        own_copy = pltpu.make_async_copy(outbuf.at[slab(0, corner)], place, out_recv)
        own_copy.start()

        def drained(count, sem):
            some = outbuf.at[pl.ds(0, count * tiles)]
            pltpu.make_async_copy(some, some, sem).wait()

        for which in range(5):
            drained(n_seq // 2 - 1, in_send.at[which, 0])
            drained(n_seq // 2, in_send.at[which, 1])
        for slot, (kind, j, group) in enumerate(ring_sent):
            whole = unit_of(kind, j, group)
            pltpu.make_async_copy(whole, whole, ring_send.at[slot]).wait()
        for copy in [queries_across] + parts_across + stats_across:
            copy.wait_send()
        drained(n_seq - 1, out_send)
        drained(n_seq, out_recv)

    return kernel


def per_device(noisy_qkv, clean_cache, span_ids, sign_bits):
    n_span, n_seq = lax.axis_size("span"), lax.axis_size("seq")
    _, rows, _, width = noisy_qkv.shape
    tiles = rows // ROW
    unit = n_seq * tiles
    tokens = unit * ROW
    ring = n_span // X_SIZE
    noisy = jnp.transpose(noisy_qkv[0], (1, 0, 2)).reshape(3, tiles, ROW, width)
    cache = jnp.transpose(clean_cache[0], (1, 0, 2)).reshape(2, tiles, ROW, width)
    vmem, anywhere = pl.BlockSpec(memory_space=pltpu.VMEM), pl.BlockSpec(memory_space=pl.ANY)
    smem = pl.BlockSpec(memory_space=pltpu.SMEM)
    dma = pltpu.SemaphoreType.DMA
    out = pl.pallas_call(
        make_kernel(n_span, n_seq, tiles, X_SIZE),
        out_shape=jax.ShapeDtypeStruct((tiles, ROW, width), BF16),
        in_specs=[vmem, smem, anywhere, anywhere],
        out_specs=anywhere,
        scratch_shapes=[
            pltpu.VMEM((2, ring + 1, unit + 1, ROW, HD), BF16),
            pltpu.VMEM((unit, ROW, HD), BF16),
            pltpu.VMEM((3, tokens + 2 * ROW, HD), BF16),
            pltpu.VMEM((ring + 1, tokens, HD), BF16),
            pltpu.VMEM((ring + 1, tokens, 2 * HD), BF16),
            pltpu.VMEM((2, tokens, HD), F32),
            pltpu.VMEM((2, tokens, HD), F32),
            pltpu.VMEM((2, tokens, HD), F32),
            pltpu.VMEM((tokens, HD), BF16),
            pltpu.VMEM((tokens, HD), BF16),
            pltpu.VMEM((N_CHUNK, 2 * ROW, HD), F32),
            pltpu.VMEM((N_CHUNK, 2 * ROW, HD), F32),
            pltpu.VMEM((unit, ROW, HD), BF16),
            dma((5, 2)), dma((5, 2)), dma((12,)), dma((2, ring, 2)),
            dma((2 * N_CHUNK + 1,)), dma((2 * N_CHUNK + 1,)), dma, dma,
        ],
        compiler_params=pltpu.CompilerParams(
            collective_id=0, has_side_effects=True, vmem_limit_bytes=50 * 2**20
        ),
        cost_estimate=pl.CostEstimate(
            flops=8 * 4 * tokens * tokens * HD, bytes_accessed=2 * 2**20,
            transcendentals=8 * tokens * tokens,
        ),
        name="span_attention",
    )(sign_bits.reshape(1, HD), span_ids, cache, noisy)
    return out.reshape(1, rows, width)


def solution(mesh):
    placed = (P("span", "seq", None, None), P("span", "seq", None, None), P("span"), P())
    return jax.shard_map(
        per_device, mesh=mesh, in_specs=placed, out_specs=P("span", "seq", None), check_vma=False
    )
```

```python
import math

import jax
import jax.numpy as jnp
from jax import lax
from jax.experimental import pallas as pl
from jax.experimental.pallas import tpu as pltpu
from jax.sharding import PartitionSpec as P

HD = 128
ROW = 8
X_SIZE = 2
N_CHUNK = 4
SPREAD = 64
LOG2E_SCALE = math.log2(math.e) / math.sqrt(HD)
HIDDEN = -1e30
OFF = 1e30
F32 = jnp.float32
BF16 = jnp.bfloat16


def turn_matrix(sign_row):
    row = lax.broadcasted_iota(jnp.int32, (HD, HD), 0)
    col = lax.broadcasted_iota(jnp.int32, (HD, HD), 1)
    both = row & col
    parity = jnp.zeros((HD, HD), jnp.int32)
    for digit in range(HD.bit_length() - 1):
        parity = parity + ((both >> digit) & 1)
    entry = 1 - 2 * (parity & 1)
    return (entry * (2 * sign_row - 1)).astype(F32).astype(BF16)


def make_kernel(n_span, n_seq, tiles, x_size):
    ring = n_span // x_size
    line = n_seq // 4
    unit = n_seq * tiles
    tokens = unit * ROW
    half_unit, half = unit // 2, tokens // 2
    n_chunk = N_CHUNK
    chunk = tokens // n_chunk
    near = ring
    per_chunk = n_seq // n_chunk
    id_rows = pl.ds(tokens, 2 * ROW)

    def kernel(
        sign_ref, id_ref, cache_ref, noisy_ref, out_ref,
        kv, qraw, sides, key_s, val_s, m_s, l_s, a_s, part_out, part_in, stat_out, stat_in, outbuf,
        in_send, in_recv, ring_send, ring_recv, x_send, x_recv, out_send, out_recv,
    ):
        span = lax.axis_index("span")
        seq = lax.axis_index("seq")
        x = span // ring
        y = span % ring
        above, below = (y + 1) % ring, (y + ring - 1) % ring
        opposite = (y + 2) % ring
        partner = ((x + 1) % x_size) * ring + y
        lane, plane = seq % 2, seq // (n_seq // 2)
        spot = seq // 2 % line
        corner = plane * 2 + lane

        def seat(distance, place):
            return place // 2 * 2 * line + lax.rem(spot + distance + line, line) * 2 + place % 2

        barrier = pltpu.get_barrier_semaphore()

        def greet(k, carry):
            pl.semaphore_signal(barrier, inc=1, device_id=(span, lax.rem(seq + k, n_seq)))
            return carry

        lax.fori_loop(1, n_seq, greet, 0)
        for target in (partner, x * ring + above, x * ring + below):
            pl.semaphore_signal(barrier, inc=1, device_id=(target, seq))
        pl.semaphore_wait(barrier, n_seq - 1 + 3)

        def columns(t):
            return pl.ds(pl.multiple_of(t * HD, HD), HD)

        def slab(first, slot):
            return pl.ds(first + slot * tiles, tiles)

        two = jnp.where(lane == 1, 2, -2)
        routes = (
            ((0, 0), (1, 8), (-1, 4), (two, 12)),
            ((4, 28), (3, 24), (-3, 20), (-two, 16)),
        )

        def scatter(src, dst, first, which, group):
            for distance, base in routes[group]:
                here = dst.at[slab(first, base + corner)]

                def send(p, carry, distance=distance, here=here):
                    t = seat(distance, lax.rem(corner + p, 4))
                    pltpu.make_async_remote_copy(
                        src_ref=src.at[:, :, columns(t)],
                        dst_ref=here,
                        send_sem=in_send.at[which, group],
                        recv_sem=in_recv.at[which, group],
                        device_id=(span, t),
                    ).start()
                    return carry

                if group == 0 and base == 0:
                    lax.fori_loop(1, 4, send, 0)
                    pltpu.make_async_copy(
                        src.at[:, :, columns(seq)], here, in_recv.at[which, group]
                    ).start()
                else:
                    lax.fori_loop(0, 4, send, 0)

        def scattered(dst, first, which, group):
            whole = dst.at[pl.ds(first + group * half_unit, half_unit)]
            pltpu.make_async_copy(whole, whole, in_recv.at[which, group]).wait()

        def scatter_pair(group):
            for distance, base in routes[group]:
                here = kv.at[:, near, slab(1, base + corner)]

                def send(p, carry, distance=distance, here=here):
                    t = seat(distance, lax.rem(corner + p, 4))
                    pltpu.make_async_remote_copy(
                        src_ref=noisy_ref.at[pl.ds(1, 2), :, :, columns(t)],
                        dst_ref=here,
                        send_sem=in_send.at[3, group],
                        recv_sem=in_recv.at[3, group],
                        device_id=(span, t),
                    ).start()
                    return carry

                if group == 0 and base == 0:
                    lax.fori_loop(1, 4, send, 0)
                    pltpu.make_async_copy(
                        noisy_ref.at[pl.ds(1, 2), :, :, columns(seq)], here, in_recv.at[3, group]
                    ).start()
                else:
                    lax.fori_loop(0, 4, send, 0)

        def unit_of(kind, j, group):
            if group == 0:
                return kv.at[kind, j, pl.ds(kind, half_unit + 1 - kind)]
            return kv.at[kind, j, pl.ds(1 + half_unit, half_unit)]

        ring_sent = []

        def pass_on(kind, j, group, target):
            pltpu.make_async_remote_copy(
                src_ref=unit_of(kind, j, group),
                dst_ref=unit_of(kind, j, group),
                send_sem=ring_send.at[len(ring_sent)],
                recv_sem=ring_recv.at[kind, j, group],
                device_id=(x * ring + target, seq),
            ).start()
            ring_sent.append((kind, j, group))

        def arrived(kind, j, group):
            whole = unit_of(kind, j, group)
            pltpu.make_async_copy(whole, whole, ring_recv.at[kind, j, group]).wait()

        def cross(src, dst, slot):
            return pltpu.make_async_remote_copy(
                src_ref=src, dst_ref=dst, send_sem=x_send.at[slot], recv_sem=x_recv.at[slot],
                device_id=(partner, seq),
            )

        queries_across = cross(sides.at[0], sides.at[2], 0)

        def rows_of(c):
            return pl.ds(c * chunk, chunk)

        parts_across = [
            cross(part_out.at[rows_of(c)], part_in.at[rows_of(c)], 1 + c) for c in range(n_chunk)
        ]
        stats_across = [
            cross(stat_out.at[c], stat_in.at[c], 1 + n_chunk + c) for c in range(n_chunk)
        ]

        scatter(cache_ref.at[0], kv.at[0, y], 1, 0, 0)
        scatter(cache_ref.at[1], kv.at[1, y], 1, 1, 0)
        scatter(noisy_ref.at[0], qraw, 0, 2, 0)
        scatter(noisy_ref.at[0], qraw, 0, 2, 1)

        my_id = jnp.full((2 * ROW, HD), id_ref[0], jnp.int32).astype(F32).astype(BF16)
        kv[0, y, 0] = my_id[:ROW]
        sides[0, id_rows] = my_id
        m_s[...] = jnp.full(m_s.shape, HIDDEN, F32)
        l_s[...] = jnp.zeros(l_s.shape, F32)
        a_s[...] = jnp.zeros(a_s.shape, F32)
        for j in range(ring + 1):
            val_s[j, :, HD:] = jnp.ones((tokens, HD), BF16)
        stat_out[...] = jnp.zeros(stat_out.shape, F32)
        turn = turn_matrix(sign_ref[...])

        scattered(kv.at[0, y], 1, 0, 0)
        pass_on(0, y, 0, above)
        pass_on(0, y, 0, below)
        scattered(kv.at[1, y], 1, 1, 0)
        pass_on(1, y, 0, above)
        pass_on(1, y, 0, below)
        scatter(cache_ref.at[0], kv.at[0, y], 1, 0, 1)
        arrived(0, below, 0)
        pass_on(0, below, 0, above)
        arrived(1, above, 0)
        pass_on(1, above, 0, below)
        scattered(qraw, 0, 2, 0)
        scattered(qraw, 0, 2, 1)
        query = qraw[...].astype(F32).reshape(tokens, HD).astype(BF16)
        sides[0, pl.ds(0, tokens)] = (
            lax.dot_general(query, turn, (((1,), (1,)), ((), ())), preferred_element_type=F32)
            * (1.0 / math.sqrt(HD))
        ).astype(BF16)
        queries_across.start()
        sides[1, pl.ds(0, tokens)] = query
        scatter(cache_ref.at[1], kv.at[1, y], 1, 1, 1)

        plan = (
            (0, above, 0), (0, below, 0), (0, opposite, 0),
            (2, y, 0), (2, above, 0), (2, below, 0), (2, opposite, 0),
            (2, y, 1), (2, above, 1), (2, below, 1), (2, opposite, 1),
            (0, above, 1), (0, below, 1), (0, opposite, 1),
        )

        def pick(i, field):
            got = plan[0][field]
            for place in range(1, len(plan)):
                got = jnp.where(i == place, plan[place][field], got)
            return got

        diagonal = lax.broadcasted_iota(jnp.int32, (SPREAD, HD), 0) == lax.broadcasted_iota(
            jnp.int32, (SPREAD, HD), 1
        )

        def loosen(j, group, size, count):
            rows = pl.ds(pl.multiple_of(group * half, half), size)
            for kind, dst in ((0, key_s), (1, val_s)):
                dst[j, rows, :HD] = (
                    kv[kind, j, pl.ds(1 + group * half_unit, count)]
                    .astype(F32).reshape(size, HD).astype(BF16)
                )

        def score(side, rows, keys):
            return lax.dot_general(
                sides[side, rows], keys, (((1,), (1,)), ((), ())), preferred_element_type=F32
            )

        def absorb(state, side, j, group, order, after):
            seen = (kv[0, j, 0].astype(F32) < sides[side, id_rows].astype(F32)[:ROW])[:1, :1]
            here = pl.ds(pl.multiple_of(group * half, half), half)
            ahead = score(side, rows_of(order[0]), key_s[j, here])
            for place, c in enumerate(order):
                rows = rows_of(c)
                scores = ahead
                if place + 1 < n_chunk:
                    ahead = score(side, rows_of(order[place + 1]), key_s[j, here])
                top = jnp.max(scores, axis=1, keepdims=True) * LOG2E_SCALE
                top = jnp.where(seen, top, HIDDEN)
                old = m_s[state, rows][:, :1]
                new = jnp.maximum(old, top)
                weights = jnp.exp2(scores * LOG2E_SCALE - jnp.where(seen, new, OFF)).astype(BF16)
                factor = jnp.exp2(old - new)
                part = jnp.dot(weights, val_s[j, here], preferred_element_type=F32)
                l_s[state, rows] = l_s[state, rows] * factor + part[:, HD:]
                a_s[state, rows] = a_s[state, rows] * factor + part[:, :HD]
                m_s[state, rows] = jnp.broadcast_to(new, (chunk, HD))
                after(c)

        def step(i, carry):
            side, j, group = pick(i, 0), pick(i, 1), pick(i, 2)

            @pl.when(i == 0)
            def _():
                arrived(0, above, 0)

            @pl.when(i == 1)
            def _():
                arrived(1, below, 0)

            @pl.when(i == 2)
            def _():
                arrived(0, opposite, 0)
                arrived(1, opposite, 0)

            @pl.when(i == 3)
            def _():
                for kind in range(2):
                    scattered(kv.at[kind, y], 1, kind, 1)
                    pass_on(kind, y, 1, above)
                    pass_on(kind, y, 1, below)
                for group in range(2):
                    scatter_pair(group)
                queries_across.wait_recv()

            @pl.when(i == 4)
            def _():
                arrived(0, below, 1)
                pass_on(0, below, 1, above)

            @pl.when(i == 6)
            def _():
                arrived(1, above, 1)
                pass_on(1, above, 1, below)

            @pl.when(i == 8)
            def _():
                arrived(0, above, 1)

            @pl.when(i == 9)
            def _():
                arrived(1, below, 1)

            @pl.when((i < 4) | (i > 6))
            def _():
                loosen(j, group, half, half_unit)

            absorb(side // 2, side, j, group, tuple(range(n_chunk)), lambda c: None)
            return carry

        lax.fori_loop(0, 10, step, 0)

        arrived(0, opposite, 1)
        arrived(1, opposite, 1)
        loosen(opposite, 1, half, half_unit)

        backward = tuple(reversed(range(n_chunk)))

        def send_part(c):
            parts_across[c].start()
            stats_across[c].start()

        def give_part(c):
            part_out[rows_of(c)] = a_s[1, rows_of(c)].astype(BF16)
            for b in range(chunk // SPREAD):
                rows = pl.ds(c * chunk + b * SPREAD, SPREAD)
                for place, stat in ((0, m_s), (ROW, l_s)):
                    stat_out[c, pl.ds(place + b, 1)] = jnp.sum(
                        jnp.where(diagonal, stat[1, rows], 0.0), axis=0, keepdims=True
                    )
            if c == backward[0]:
                send_part(c)
            if c == backward[-1]:
                send_part(backward[1])

        absorb(1, 2, opposite, 1, backward, give_part)

        def own_step(i, carry):
            for place in range(2, n_chunk):

                @pl.when(i == 10 + place)
                def _(place=place):
                    send_part(backward[place])

            absorb(0, 0, pick(i, 1), 1, tuple(range(n_chunk)), lambda c: None)
            return carry

        lax.fori_loop(11, len(plan), own_step, 0)

        pair = kv.at[:, near, pl.ds(1, unit)]
        for group in range(2):
            some = pair.at[:, pl.ds(group * half_unit, half_unit)]
            pltpu.make_async_copy(some, some, in_recv.at[3, group]).wait()
        loosen(near, 0, tokens, unit)
        place = out_ref.at[:, :, columns(seq)]

        def give(slot, t):
            pltpu.make_async_remote_copy(
                src_ref=outbuf.at[slab(0, slot)], dst_ref=place,
                send_sem=out_send, recv_sem=out_recv, device_id=(span, t),
            ).start()

        back = ((0, 0), (1, 1), (-1, -1), (2, -2), (-2, 2), (3, 3), (-3, -3), (4, 4))
        ahead = score(1, pl.ds((n_chunk - 1) * chunk, chunk), key_s[near])
        for c in backward:
            rows = rows_of(c)
            scores = ahead
            if c > 0:
                ahead = score(1, pl.ds((c - 1) * chunk, chunk), key_s[near])
            top = jnp.max(scores, axis=1, keepdims=True) * LOG2E_SCALE
            weights = jnp.exp2(scores * LOG2E_SCALE - top).astype(BF16)
            part = jnp.dot(weights, val_s[near], preferred_element_type=F32)
            parts_across[c].wait_recv()
            stats_across[c].wait_recv()
            for b in range(chunk // SPREAD):
                some = pl.ds(c * chunk + b * SPREAD, SPREAD)
                for start, stat in ((0, m_s), (ROW, l_s)):
                    spread = jnp.broadcast_to(stat_in[c, pl.ds(start + b, 1)], (SPREAD, HD))
                    stat[1, some] = jnp.broadcast_to(
                        jnp.sum(jnp.where(diagonal, spread, 0.0), axis=1, keepdims=True),
                        (SPREAD, HD),
                    )
            best = jnp.maximum(jnp.maximum(m_s[0, rows], m_s[1, rows]), top)
            far_factor = jnp.exp2(m_s[0, rows] - best)
            near_factor = jnp.exp2(top - best)
            across_factor = jnp.exp2(m_s[1, rows] - best)
            far = a_s[0, rows] * far_factor + part_in[rows].astype(F32) * across_factor
            high = far.astype(BF16)
            low = (far - high.astype(F32)).astype(BF16)
            turned = (
                jnp.dot(high, turn, preferred_element_type=F32)
                + jnp.dot(low, turn, preferred_element_type=F32)
            ) * (1.0 / math.sqrt(HD))
            total = (
                l_s[0, rows] * far_factor + part[:, HD:] * near_factor + l_s[1, rows] * across_factor
            )
            result = (part[:, :HD] * near_factor + turned) / total
            outbuf[pl.ds(c * per_chunk * tiles, per_chunk * tiles)] = (
                result.reshape(per_chunk * tiles, ROW, HD).astype(BF16)
            )

            @pl.when(seq >= 0)
            def _(c=c):
                for g in reversed(range(2 * c, 2 * c + 2)):
                    for p in range(4):
                        if g > 0:
                            give(4 * g + p, seat(back[g][p % 2], p))
                        elif p > 0:
                            other = lax.rem(corner + p, 4)
                            give(other, seat(0, other))

        own_copy = pltpu.make_async_copy(outbuf.at[slab(0, corner)], place, out_recv)
        own_copy.start()

        def drained(count, sem):
            some = outbuf.at[pl.ds(0, count * tiles)]
            pltpu.make_async_copy(some, some, sem).wait()

        for which in range(3):
            drained(n_seq // 2 - 1, in_send.at[which, 0])
            drained(n_seq // 2, in_send.at[which, 1])
        for group in range(2):
            some = kv.at[:, near, pl.ds(1, (n_seq // 2 - 1 + group) * tiles)]
            pltpu.make_async_copy(some, some, in_send.at[3, group]).wait()
        for slot, (kind, j, group) in enumerate(ring_sent):
            whole = unit_of(kind, j, group)
            pltpu.make_async_copy(whole, whole, ring_send.at[slot]).wait()
        for copy in [queries_across] + parts_across + stats_across:
            copy.wait_send()
        drained(n_seq - 1, out_send)
        drained(n_seq, out_recv)

    return kernel


def per_device(noisy_qkv, clean_cache, span_ids, sign_bits):
    n_span, n_seq = lax.axis_size("span"), lax.axis_size("seq")
    _, rows, _, width = noisy_qkv.shape
    tiles = rows // ROW
    unit = n_seq * tiles
    tokens = unit * ROW
    ring = n_span // X_SIZE
    noisy = jnp.transpose(noisy_qkv[0], (1, 0, 2)).reshape(3, tiles, ROW, width)
    cache = jnp.transpose(clean_cache[0], (1, 0, 2)).reshape(2, tiles, ROW, width)
    vmem, anywhere = pl.BlockSpec(memory_space=pltpu.VMEM), pl.BlockSpec(memory_space=pl.ANY)
    smem = pl.BlockSpec(memory_space=pltpu.SMEM)
    dma = pltpu.SemaphoreType.DMA
    out = pl.pallas_call(
        make_kernel(n_span, n_seq, tiles, X_SIZE),
        out_shape=jax.ShapeDtypeStruct((tiles, ROW, width), BF16),
        in_specs=[vmem, smem, anywhere, anywhere],
        out_specs=anywhere,
        scratch_shapes=[
            pltpu.VMEM((2, ring + 1, unit + 1, ROW, HD), BF16),
            pltpu.VMEM((unit, ROW, HD), BF16),
            pltpu.VMEM((3, tokens + 2 * ROW, HD), BF16),
            pltpu.VMEM((ring + 1, tokens, HD), BF16),
            pltpu.VMEM((ring + 1, tokens, 2 * HD), BF16),
            pltpu.VMEM((2, tokens, HD), F32),
            pltpu.VMEM((2, tokens, HD), F32),
            pltpu.VMEM((2, tokens, HD), F32),
            pltpu.VMEM((tokens, HD), BF16),
            pltpu.VMEM((tokens, HD), BF16),
            pltpu.VMEM((N_CHUNK, 2 * ROW, HD), F32),
            pltpu.VMEM((N_CHUNK, 2 * ROW, HD), F32),
            pltpu.VMEM((unit, ROW, HD), BF16),
            dma((4, 2)), dma((4, 2)), dma((12,)), dma((2, ring, 2)),
            dma((2 * N_CHUNK + 1,)), dma((2 * N_CHUNK + 1,)), dma, dma,
        ],
        compiler_params=pltpu.CompilerParams(
            collective_id=0, has_side_effects=True, vmem_limit_bytes=50 * 2**20
        ),
        cost_estimate=pl.CostEstimate(
            flops=8 * 4 * tokens * tokens * HD, bytes_accessed=2 * 2**20,
            transcendentals=8 * tokens * tokens,
        ),
        name="span_attention",
    )(sign_bits.reshape(1, HD), span_ids, cache, noisy)
    return out.reshape(1, rows, width)


def solution(mesh):
    placed = (P("span", "seq", None, None), P("span", "seq", None, None), P("span"), P())
    return jax.shard_map(
        per_device, mesh=mesh, in_specs=placed, out_specs=P("span", "seq", None), check_vma=False
    )
```
